32 devices in a mesh: dp: 4 (over y, x), space: 8 (over z, core).
Axes of the slice: x: 2, y: 2, z: 4, core: 2. Of those that a mesh axis runs over, the one named last changes fastest.
Arguments:
- volume: bfloat16 [4, 64, 16, 4096], P('dp', None, 'space'), may hold values from -6 to 6
- kernel_in: bfloat16 [1728, 128], replicated, may hold values from -0.15625 to 0.15625
- kernel_out: bfloat16 [3456, 128], P(None, 'space'), may hold values from -0.4375 to 0.4375
- cotangent: bfloat16 [4, 128, 8, 1024], P('dp', 'space'), may hold values from -24 to 24
Outputs:
- activation: bfloat16 [4, 128, 8, 1024], P('dp', 'space')
- volume_grad: bfloat16 [4, 64, 16, 4096], P('dp', None, 'space')
- first_grad: float32 [1728, 128], replicated
- second_grad: float32 [3456, 128], P(None, 'space')
The draws below stay inside these ranges and needn't reach their ends.
All inputs are finite; a program needn't handle non-finite values.
Results may differ from the reference program's by a relative error of at most 0.02.
Values may be sent and summed in bfloat16 or wider, within the bound.
A program may use at most 128 MiB of HBM per device.

```python
import math
import jax
import jax.numpy as jnp
from jax import lax

C0 = 64
C1 = 128
C2 = 128
SIDE = 64
SAMPLES = 4
NZ = 16


def block_levels(rng, extent, cuts, smallest, largest):
    def one(axis_at, shards_of):
        heights = jax.random.uniform(jax.random.fold_in(jax.random.fold_in(rng, 6), axis_at), (shards_of,), jnp.float32, smallest / len(cuts), largest / len(cuts))
        return jnp.repeat(jnp.exp(heights), extent[axis_at] // shards_of).reshape((-1,) + (1,) * (len(extent) - axis_at - 1))

    level = one(*cuts[0])
    for cut in cuts[1:]:
        level = level * one(*cut)
    return level


def bell_draw(rng, shape, scale, bound, cuts=(), kind=jnp.bfloat16):
    gain = block_levels(rng, shape, cuts, -0.22, 0.18) if cuts else 1.0
    drawn = jax.random.normal(rng, shape, jnp.float32) * scale * gain
    return jnp.minimum(jnp.maximum(drawn, -bound), bound).astype(kind)


def setup_inputs(seed: int = 0) -> dict:
    splits = jax.random.split(jax.random.key(seed), 5)
    volume = bell_draw(splits[0], (SAMPLES, C0, NZ, SIDE * SIDE), 1.0, 6.0, ((0, 4), (2, 8)))
    kernel_in = bell_draw(splits[1], (27 * C0, C1), (27 * C0) ** -0.5, 0.15625)
    kernel_out = bell_draw(splits[2], (27 * C1, C2), (27 * C1 // 16) ** -0.5, 0.4375, ((1, 8),))
    cotangent = bell_draw(splits[3], (SAMPLES, C2, NZ // 2, SIDE * SIDE // 4), 4.0, 24.0, ((0, 4), (1, 8)))
    return {"volume": volume, "kernel_in": kernel_in, "kernel_out": kernel_out, "cotangent": cotangent}


LAYOUT = ('NCDHW', 'DHWIO', 'NCDHW')

def correlate(tensor, kernel):
    return lax.conv_general_dilated(tensor, kernel, (1, 1, 1), ((1, 1), (1, 1), (1, 1)), dimension_numbers=LAYOUT, precision=lax.Precision.HIGHEST)

def silu_slope(values):
    sigma = jax.nn.sigmoid(values)
    return sigma * (1.0 + values * (1.0 - sigma))

def average_pool(tensor):
    dims = tensor.shape
    return tensor.reshape(dims[0], dims[1], dims[2] // 2, 2, dims[3] // 2, 2, dims[4] // 2, 2).mean(axis=(3, 5, 7))

def spread_back(tensor):
    dims = tensor.shape
    wide = jnp.broadcast_to(tensor[:, :, :, None, :, None, :, None], (dims[0], dims[1], dims[2], 2, dims[3], 2, dims[4], 2))
    return wide.reshape(dims[0], dims[1], 2 * dims[2], 2 * dims[3], 2 * dims[4]) * 0.125

def reference(volume, kernel_in, kernel_out, cotangent):
    half_side = SIDE // 2
    kernel_first = kernel_in.astype(jnp.float32).reshape(3, 3, 3, C0, C1)
    kernel_second = kernel_out.astype(jnp.float32).reshape(3, 3, 3, C1, C2)

    def per_sample(item):
        sample, sample_cot = item
        sample_vol = sample.astype(jnp.float32).reshape(1, C0, NZ, SIDE, SIDE)
        pre_first = correlate(sample_vol, kernel_first)
        pooled = lax.optimization_barrier(average_pool(jax.nn.silu(pre_first)).astype(jnp.bfloat16)).astype(jnp.float32)
        pre_second = correlate(pooled, kernel_second)
        activation = jax.nn.silu(pre_second).astype(jnp.bfloat16)
        cot_field = sample_cot.astype(jnp.float32).reshape(1, C2, NZ // 2, half_side, half_side)
        slopes_second = lax.optimization_barrier((cot_field * silu_slope(pre_second)).astype(jnp.bfloat16)).astype(jnp.float32)
        unused_second, pull_second = jax.vjp(correlate, pooled, kernel_second)
        pooled_slope, second_term = pull_second(slopes_second)
        first_slopes = lax.optimization_barrier((spread_back(pooled_slope) * silu_slope(pre_first)).astype(jnp.bfloat16)).astype(jnp.float32)
        unused_first, pull_first = jax.vjp(correlate, sample_vol, kernel_first)
        volume_term, first_term = pull_first(first_slopes)
        return (activation.reshape(C2, NZ // 2, half_side * half_side), volume_term.astype(jnp.bfloat16).reshape(C0, NZ, SIDE * SIDE), first_term.reshape(27 * C0, C1), second_term.reshape(27 * C1, C2))
    activation, volume_grad, first_terms, second_terms = lax.map(per_sample, (volume, cotangent))
    cell_count = SAMPLES * NZ * SIDE * SIDE
    first_grad = lax.optimization_barrier(jnp.sum(first_terms, axis=0)) * (1.0 / math.sqrt(cell_count))
    second_grad = lax.optimization_barrier(jnp.sum(second_terms, axis=0)) * (1.0 / math.sqrt(cell_count // 8))
    return (activation, volume_grad, first_grad, second_grad)
```

```python
import functools
import math

import jax
import jax.numpy as jnp
from jax import lax
from jax.experimental import pallas as pl
from jax.experimental.pallas import tpu as pltpu
from jax.sharding import PartitionSpec as P

BF = jnp.bfloat16
F32 = jnp.float32
LIMIT = 56 * 1024 * 1024


def conv_body(side, tile, x_ref, k_ref, o_ref):
    base = pl.program_id(0) * tile
    total = None
    for plane in range(x_ref.shape[0]):
        for dy in range(3):
            start = pl.multiple_of(base + dy * side, 32)
            term = jnp.dot(
                x_ref[plane, pl.ds(start, tile), :],
                k_ref[plane * 3 + dy],
                preferred_element_type=F32,
            )
            total = term if total is None else total + term
    o_ref[...] = total


def conv(wide, blocks, side):
    planes, rows, depth = wide.shape
    count, _, outs = blocks.shape
    cells = side * side
    tile = min(512, cells)
    return pl.pallas_call(
        functools.partial(conv_body, side, tile),
        grid=(cells // tile,),
        in_specs=[
            pl.BlockSpec((planes, rows, depth), lambda i: (0, 0, 0)),
            pl.BlockSpec((count, depth, outs), lambda i: (0, 0, 0)),
        ],
        out_specs=pl.BlockSpec((tile, outs), lambda i: (i, 0)),
        out_shape=jax.ShapeDtypeStruct((cells, outs), F32),
        compiler_params=pltpu.CompilerParams(vmem_limit_bytes=LIMIT),
        cost_estimate=pl.CostEstimate(
            flops=2 * cells * count * depth * outs,
            bytes_accessed=2 * planes * rows * depth + 4 * cells * outs,
            transcendentals=0,
        ),
    )(wide, blocks)


def grad_body(side, s_ref, x_ref, o_ref):
    cells = s_ref.shape[1]
    tile = min(1024, cells)
    shift = pl.program_id(1) * side
    total = None
    for at in range(0, cells, tile):
        start = pl.multiple_of(shift + at, 32)
        term = jnp.dot(
            s_ref[:, at : at + tile],
            x_ref[0, pl.ds(start, tile), :],
            preferred_element_type=F32,
        )
        total = term if total is None else total + term
    o_ref[0, 0] = total


def grad(slopes, wide, side):
    planes, rows, depth = wide.shape
    chans, cells = slopes.shape
    return pl.pallas_call(
        functools.partial(grad_body, side),
        grid=(planes, 3),
        in_specs=[
            pl.BlockSpec((chans, cells), lambda p, d: (0, 0)),
            pl.BlockSpec((1, rows, depth), lambda p, d: (p, 0, 0)),
        ],
        out_specs=pl.BlockSpec((1, 1, chans, depth), lambda p, d: (p, d, 0, 0)),
        out_shape=jax.ShapeDtypeStruct((planes, 3, chans, depth), F32),
        compiler_params=pltpu.CompilerParams(vmem_limit_bytes=LIMIT),
        cost_estimate=pl.CostEstimate(
            flops=2 * cells * planes * 3 * depth * chans,
            bytes_accessed=2 * planes * rows * depth + 12 * planes * chans * depth,
            transcendentals=0,
        ),
    )(slopes, wide)


def kernel_gradient(slopes, wide, side, slabs):
    parts = grad(slopes.T, wide, side)
    chans = slopes.shape[1] // slabs
    total = sum(
        parts[z : z + 3, :, z * chans : (z + 1) * chans, :] for z in range(slabs)
    )
    return jnp.transpose(total, (2, 0, 1, 3)).reshape(chans, -1)


def widen(planes, side):
    count, _, chans = planes.shape
    grid = jnp.pad(
        planes.reshape(count, side, side, chans), ((0, 0), (1, 1), (1, 1), (0, 0))
    )
    wide = jnp.concatenate([grid[:, :, d : d + side, :] for d in range(3)], axis=3)
    return wide.reshape(count, (side + 2) * side, 3 * chans)


def block_kernel(kernel, slabs):
    ins, outs = kernel.shape[3], kernel.shape[4]
    flat = kernel.reshape(3, 3, 3 * ins, outs)
    columns = [
        jnp.pad(flat, ((z, slabs - 1 - z), (0, 0), (0, 0), (0, 0))) for z in range(slabs)
    ]
    return jnp.concatenate(columns, axis=3).reshape((slabs + 2) * 3, 3 * ins, slabs * outs)


def reverse_kernel(kernel):
    return jnp.swapaxes(jnp.flip(kernel, (0, 1, 2)), 3, 4)


def silu_slope(values):
    sigma = jax.nn.sigmoid(values)
    return sigma * (1.0 + values * (1.0 - sigma))


def neighbours(first, last):
    count = lax.axis_size("space")
    before = lax.ppermute(last, "space", [(i, i + 1) for i in range(count - 1)])
    after = lax.ppermute(first, "space", [(i + 1, i) for i in range(count - 1)])
    return before, after


def extend(planes):
    before, after = neighbours(planes[:1], planes[-1:])
    return jnp.concatenate([before, planes, after], axis=0)


def owner_sum(local):
    count = lax.axis_size("space")
    chans, width = local.shape
    sent = local.astype(BF).reshape(count, chans // count, width)
    got = lax.all_to_all(sent, "space", split_axis=0, concat_axis=0, tiled=True)
    mine = jnp.sum(got.astype(F32), axis=0).astype(BF)
    groups = lax.all_gather(mine, "dp", axis=0, tiled=False)
    return jnp.sum(groups.astype(F32), axis=0)


def per_device(volume, kernel_in, kernel_out, cotangent):
    in_chan, slabs, area = volume.shape[1:]
    mid_chan = kernel_in.shape[1]
    side = math.isqrt(area)
    half = side // 2
    thin = slabs // 2
    full_kernel = lax.all_gather(kernel_out, "space", axis=1, tiled=True)
    all_out = full_kernel.shape[1]
    slab_cot = lax.all_to_all(cotangent, "space", split_axis=2, concat_axis=1, tiled=True)
    kernel_first = kernel_in.reshape(3, 3, 3, in_chan, mid_chan)
    kernel_second = full_kernel.reshape(3, 3, 3, mid_chan, all_out)

    planes = jnp.swapaxes(volume[0], 0, 1)
    before, after = neighbours(planes[:1], planes[-1:])
    planes = jnp.concatenate([before, planes, after], axis=0)
    volume_wide = widen(jnp.swapaxes(planes, 1, 2), side)
    pre_first = conv(volume_wide, block_kernel(kernel_first, slabs), side)
    pooled = (
        jax.nn.silu(pre_first)
        .reshape(half, 2, half, 2, thin, 2, mid_chan)
        .mean(axis=(1, 3, 5))
        .astype(BF)
    )
    pooled = jnp.transpose(pooled, (2, 0, 1, 3)).reshape(thin, half * half, mid_chan)
    pooled_wide = widen(extend(pooled), half)
    pre_second = conv(pooled_wide, block_kernel(kernel_second, thin), half)
    slab_act = jax.nn.silu(pre_second).astype(BF).T.reshape(thin, all_out, half * half)
    activation = lax.all_to_all(
        jnp.swapaxes(slab_act, 0, 1)[None], "space", split_axis=1, concat_axis=2, tiled=True
    )
    cells_cot = jnp.transpose(slab_cot[0], (2, 1, 0)).reshape(half * half, thin * all_out)
    slopes_second = (cells_cot.astype(F32) * silu_slope(pre_second)).astype(BF)
    second_planes = jnp.swapaxes(slopes_second.reshape(half * half, thin, all_out), 0, 1)
    second_wide = widen(extend(second_planes), half)
    second_sum = owner_sum(kernel_gradient(slopes_second, pooled_wide, half, thin))
    pooled_slope = conv(second_wide, block_kernel(reverse_kernel(kernel_second), thin), half)
    spread = jnp.broadcast_to(
        pooled_slope.reshape(half, 1, half, 1, thin, 1, mid_chan),
        (half, 2, half, 2, thin, 2, mid_chan),
    ).reshape(area, slabs * mid_chan)
    first_slopes = (spread * 0.125 * silu_slope(pre_first)).astype(BF)
    first_mine = owner_sum(kernel_gradient(first_slopes, volume_wide, side, slabs))
    first_planes = jnp.stack(
        [first_slopes[:, z * mid_chan : (z + 1) * mid_chan] for z in range(slabs)]
    )
    first_wide = widen(extend(first_planes), side)
    volume_grad = conv(first_wide, block_kernel(reverse_kernel(kernel_first), slabs), side)
    volume_grad = volume_grad.astype(BF).T.reshape(slabs, in_chan, area)
    volume_grad = jnp.swapaxes(volume_grad, 0, 1)[None]
    first_sum = lax.all_gather(first_mine.astype(BF), "space", axis=0, tiled=True)
    cell_count = (
        volume.shape[0] * lax.axis_size("dp") * slabs * lax.axis_size("space") * area
    )
    first_grad = first_sum.T.astype(F32) * (1.0 / math.sqrt(cell_count))
    second_grad = second_sum.T * (1.0 / math.sqrt(cell_count // 8))
    return (activation, volume_grad, first_grad, second_grad)


def solution(mesh):
    return jax.shard_map(
        per_device,
        mesh=mesh,
        in_specs=(
            P("dp", None, "space", None),
            P(),
            P(None, "space"),
            P("dp", "space", None, None),
        ),
        out_specs=(
            P("dp", "space", None, None),
            P("dp", None, "space", None),
            P(),
            P(None, "space"),
        ),
        check_vma=False,
    )
```

```python
import functools
import math

import jax
import jax.numpy as jnp
from jax import lax
from jax.experimental import pallas as pl
from jax.experimental.pallas import tpu as pltpu
from jax.sharding import PartitionSpec as P

BF = jnp.bfloat16
F32 = jnp.float32
LIMIT = 56 * 1024 * 1024


def convolved(side, tile, x_ref, k_ref):
    base = pl.program_id(0) * tile
    total = None
    for plane in range(x_ref.shape[0]):
        for dy in range(3):
            start = pl.multiple_of(base + dy * side, 32)
            term = jnp.dot(
                x_ref[plane, pl.ds(start, tile), :],
                k_ref[plane * 3 + dy],
                preferred_element_type=F32,
            )
            total = term if total is None else total + term
    return total


def plain_body(side, tile, x_ref, k_ref, o_ref):
    o_ref[...] = convolved(side, tile, x_ref, k_ref).astype(o_ref.dtype)


def pool_body(side, tile, x_ref, k_ref, slope_ref, pooled_ref, held):
    total = convolved(side, tile, x_ref, k_ref)
    sigma = jax.nn.sigmoid(total)
    slope_ref[...] = 0.125 * (sigma * (1.0 + total * (1.0 - sigma)))
    act = total * sigma
    thin, few, chans = pooled_ref.shape
    for z in range(thin):
        low = act[:, 2 * z * chans : (2 * z + 1) * chans]
        high = act[:, (2 * z + 1) * chans : (2 * z + 2) * chans]
        rows = (low + high).reshape(tile // (2 * side), 2, side, chans)
        held[...] = (rows[:, 0] + rows[:, 1]).reshape(tile // 2, chans)
        mean = held[pl.ds(0, few, stride=2), :] + held[pl.ds(1, few, stride=2), :]
        pooled_ref[z] = (mean * 0.125).astype(BF)


def spread_body(side, tile, x_ref, k_ref, slope_ref, o_ref, held):
    total = convolved(side, tile, x_ref, k_ref)
    slabs, many, chans = o_ref.shape
    for z in range(slabs // 2):
        part = total[:, z * chans : (z + 1) * chans]
        held[pl.ds(0, tile, stride=2), :] = part
        held[pl.ds(1, tile, stride=2), :] = part
        rows = held[...].reshape(tile // side, 1, 2 * side, chans)
        wide = jnp.concatenate([rows, rows], axis=1).reshape(many, chans)
        for plane in (2 * z, 2 * z + 1):
            slope = slope_ref[:, plane * chans : (plane + 1) * chans]
            o_ref[plane] = (wide * slope).astype(BF)


def call_conv(body, wide, blocks, side, extra, extra_specs, outs, out_specs, scratch):
    planes, rows, depth = wide.shape
    count, _, width = blocks.shape
    cells = side * side
    tile = min(512, cells)
    return pl.pallas_call(
        functools.partial(body, side, tile),
        grid=(cells // tile,),
        in_specs=[
            pl.BlockSpec((planes, rows, depth), lambda i: (0, 0, 0)),
            pl.BlockSpec((count, depth, width), lambda i: (0, 0, 0)),
            *extra_specs(tile),
        ],
        out_specs=out_specs(tile),
        out_shape=outs,
        scratch_shapes=scratch(tile),
        compiler_params=pltpu.CompilerParams(vmem_limit_bytes=LIMIT),
        cost_estimate=pl.CostEstimate(
            flops=2 * cells * count * depth * width,
            bytes_accessed=2 * planes * rows * depth + 4 * cells * width,
            transcendentals=0,
        ),
    )(wide, blocks, *extra)


def conv(wide, blocks, side, dtype):
    width = blocks.shape[2]
    return call_conv(
        plain_body, wide, blocks, side, (), lambda tile: [],
        jax.ShapeDtypeStruct((side * side, width), dtype),
        lambda tile: pl.BlockSpec((tile, width), lambda i: (i, 0)),
        lambda tile: [],
    )


def conv_pool(wide, blocks, side, slabs):
    width = blocks.shape[2]
    chans, thin, cells = width // slabs, slabs // 2, side * side
    return call_conv(
        pool_body, wide, blocks, side, (), lambda tile: [],
        [
            jax.ShapeDtypeStruct((cells, width), F32),
            jax.ShapeDtypeStruct((thin, cells // 4, chans), BF),
        ],
        lambda tile: [
            pl.BlockSpec((tile, width), lambda i: (i, 0)),
            pl.BlockSpec((thin, tile // 4, chans), lambda i: (0, i, 0)),
        ],
        lambda tile: [pltpu.VMEM((tile // 2, chans), F32)],
    )


def conv_spread(wide, blocks, side, slope, slabs):
    cells, width = slope.shape
    chans = width // slabs
    return call_conv(
        spread_body, wide, blocks, side, (slope,),
        lambda tile: [pl.BlockSpec((4 * tile, width), lambda i: (i, 0))],
        jax.ShapeDtypeStruct((slabs, cells, chans), BF),
        lambda tile: pl.BlockSpec((slabs, 4 * tile, chans), lambda i: (0, i, 0)),
        lambda tile: [pltpu.VMEM((2 * tile, chans), F32)],
    )


def grad_body(side, s_ref, x_ref, o_ref):
    cells = s_ref.shape[1]
    tile = min(1024, cells)
    shift = pl.program_id(1) * side
    total = None
    for at in range(0, cells, tile):
        start = pl.multiple_of(shift + at, 32)
        term = jnp.dot(
            s_ref[:, at : at + tile],
            x_ref[0, pl.ds(start, tile), :],
            preferred_element_type=F32,
        )
        total = term if total is None else total + term
    o_ref[0, 0] = total


def grad(slopes, wide, side):
    planes, rows, depth = wide.shape
    chans, cells = slopes.shape
    return pl.pallas_call(
        functools.partial(grad_body, side),
        grid=(planes, 3),
        in_specs=[
            pl.BlockSpec((chans, cells), lambda p, d: (0, 0)),
            pl.BlockSpec((1, rows, depth), lambda p, d: (p, 0, 0)),
        ],
        out_specs=pl.BlockSpec((1, 1, chans, depth), lambda p, d: (p, d, 0, 0)),
        out_shape=jax.ShapeDtypeStruct((planes, 3, chans, depth), F32),
        compiler_params=pltpu.CompilerParams(vmem_limit_bytes=LIMIT),
        cost_estimate=pl.CostEstimate(
            flops=2 * cells * planes * 3 * depth * chans,
            bytes_accessed=2 * planes * rows * depth + 12 * planes * chans * depth,
            transcendentals=0,
        ),
    )(slopes, wide)


def kernel_gradient(planes, wide, side):
    slabs, cells, chans = planes.shape
    parts = grad(jnp.swapaxes(planes, 1, 2).reshape(slabs * chans, cells), wide, side)
    total = sum(
        parts[z : z + 3, :, z * chans : (z + 1) * chans, :] for z in range(slabs)
    )
    return jnp.transpose(total, (2, 0, 1, 3)).reshape(chans, -1)


def widen(planes, side):
    count, _, chans = planes.shape
    grid = jnp.pad(
        planes.reshape(count, side, side, chans), ((0, 0), (1, 1), (1, 1), (0, 0))
    )
    wide = jnp.concatenate([grid[:, :, d : d + side, :] for d in range(3)], axis=3)
    return wide.reshape(count, (side + 2) * side, 3 * chans)


def block_kernel(kernel, slabs):
    ins, outs = kernel.shape[3], kernel.shape[4]
    flat = kernel.reshape(3, 3, 3 * ins, outs)
    columns = [
        jnp.pad(flat, ((z, slabs - 1 - z), (0, 0), (0, 0), (0, 0))) for z in range(slabs)
    ]
    return jnp.concatenate(columns, axis=3).reshape((slabs + 2) * 3, 3 * ins, slabs * outs)


def reverse_kernel(kernel):
    return jnp.swapaxes(jnp.flip(kernel, (0, 1, 2)), 3, 4)


def silu_slope(values):
    sigma = jax.nn.sigmoid(values)
    return sigma * (1.0 + values * (1.0 - sigma))


def neighbours(first, last):
    count = lax.axis_size("space")
    before = lax.ppermute(last, "space", [(i, i + 1) for i in range(count - 1)])
    after = lax.ppermute(first, "space", [(i + 1, i) for i in range(count - 1)])
    return before, after


def extend(planes):
    before, after = neighbours(planes[:1], planes[-1:])
    return jnp.concatenate([before, planes, after], axis=0)


def gathered(mine, axis):
    count = lax.axis_size(axis)
    copies = jnp.broadcast_to(mine[None], (count, *mine.shape))
    return lax.all_to_all(copies, axis, split_axis=0, concat_axis=0, tiled=True)


def owner_sum(local):
    count = lax.axis_size("space")
    chans, width = local.shape
    sent = local.astype(BF).reshape(count, chans // count, width)
    got = lax.all_to_all(sent, "space", split_axis=0, concat_axis=0, tiled=True)
    return jnp.sum(got.astype(F32), axis=0).astype(BF)


def per_device(volume, kernel_in, kernel_out, cotangent):
    in_chan, slabs, area = volume.shape[1:]
    mid_chan = kernel_in.shape[1]
    side = math.isqrt(area)
    half = side // 2
    thin = slabs // 2
    full_kernel = gathered(kernel_out.T, "space").reshape(-1, kernel_out.shape[0]).T
    all_out = full_kernel.shape[1]
    slab_cot = lax.all_to_all(cotangent, "space", split_axis=2, concat_axis=1, tiled=True)
    kernel_first = kernel_in.reshape(3, 3, 3, in_chan, mid_chan)
    kernel_second = full_kernel.reshape(3, 3, 3, mid_chan, all_out)

    planes = extend(jnp.swapaxes(volume[0], 0, 1))
    volume_wide = widen(jnp.swapaxes(planes, 1, 2), side)
    slope_first, pooled = conv_pool(volume_wide, block_kernel(kernel_first, slabs), side, slabs)
    pooled_wide = widen(extend(pooled), half)
    pre_second = conv(pooled_wide, block_kernel(kernel_second, thin), half, F32)
    slab_act = jax.nn.silu(pre_second).astype(BF).T.reshape(thin, all_out, half * half)
    activation = lax.all_to_all(
        jnp.swapaxes(slab_act, 0, 1)[None], "space", split_axis=1, concat_axis=2, tiled=True
    )
    cells_cot = jnp.transpose(slab_cot[0], (2, 1, 0)).reshape(half * half, thin * all_out)
    slopes_second = (cells_cot.astype(F32) * silu_slope(pre_second)).astype(BF)
    second_planes = jnp.swapaxes(slopes_second.reshape(half * half, thin, all_out), 0, 1)
    second_wide = widen(extend(second_planes), half)
    second_mine = owner_sum(kernel_gradient(second_planes, pooled_wide, half))
    first_planes = conv_spread(
        second_wide,
        block_kernel(reverse_kernel(kernel_second), thin),
        half,
        slope_first,
        slabs,
    )
    first_mine = owner_sum(kernel_gradient(first_planes, volume_wide, side))
    mine = gathered(jnp.concatenate([first_mine, second_mine], axis=1), "dp")
    mine = jnp.sum(mine.astype(F32), axis=0)
    split = first_mine.shape[1]
    first_sum = gathered(mine[:, :split].astype(BF), "space").reshape(mid_chan, split)
    second_sum = mine[:, split:]
    first_wide = widen(extend(first_planes), side)
    volume_grad = conv(first_wide, block_kernel(reverse_kernel(kernel_first), slabs), side, BF)
    volume_grad = jnp.swapaxes(volume_grad.T.reshape(slabs, in_chan, area), 0, 1)[None]
    cell_count = (
        volume.shape[0] * lax.axis_size("dp") * slabs * lax.axis_size("space") * area
    )
    first_grad = first_sum.T.astype(F32) * (1.0 / math.sqrt(cell_count))
    second_grad = second_sum.T * (1.0 / math.sqrt(cell_count // 8))
    return (activation, volume_grad, first_grad, second_grad)


def solution(mesh):
    return jax.shard_map(
        per_device,
        mesh=mesh,
        in_specs=(
            P("dp", None, "space", None),
            P(),
            P(None, "space"),
            P("dp", "space", None, None),
        ),
        out_specs=(
            P("dp", "space", None, None),
            P("dp", None, "space", None),
            P(),
            P(None, "space"),
        ),
        check_vma=False,
    )
```
